128 devices in a mesh: clu: 32 (over z, x, core), row: 4 (over y).
Axes of the slice: x: 4, y: 4, z: 4, core: 2. Of those that a mesh axis runs over, the one named last changes fastest.
Arguments:
- embeddings: bfloat16 [524288, 1024], P(('clu', 'row')), may hold values from -8 to 8
- cluster_keys: int32 [524288], P(('clu', 'row')), may hold values from 0 to 127, as said below
- owner_map: int32 [128], replicated, may hold values from 0 to 127, as said below
- live_counts: int32 [128, 32], P(('clu', 'row')), may hold values from 0 to 128, as said below
- sub_centroids: bfloat16 [128, 256, 1024], P('clu'), may hold values from -6 to 6
Outputs:
- new_centroids: float32 [128, 256, 1024], P('clu', None, 'row')
- row_costs: float32 [524288], P(('clu', 'row'))
The draws below stay inside these ranges and needn't reach their ends.
Inputs may be any that keep to these rules, and one draw needn't show every extreme that they name: For every live slot of block j, owner_map[cluster_keys] // 4 equals j. `owner_map`: A permutation of the cluster positions. `live_counts`: every device has a full block for some owner.
All inputs are finite; a program needn't handle non-finite values.
Results may differ from the reference program's by a relative error of at most 0.00098.
Values may be sent and summed in bfloat16 or wider, within the bound.
No kernel may reach another device: no remote copies, remote signals or barrier semaphores. Data moves between devices by JAX's collectives and lax.ppermute only.
A program may use at most 128 MiB of HBM per device.

```python
import jax
import jax.numpy as jnp
from jax import lax

D = 1024
K2 = 256
CLU_DEV = 4
ROW_DEV = 4096
K1 = 128
CAP = 128
ROWS = 524288
N_CLU = 32
N_ROW = 4


def shared_order(key):
    perm = jax.random.permutation(key, K1).astype(jnp.int32)
    inverse = jnp.zeros((K1,), jnp.int32).at[perm].set(jnp.arange(K1, dtype=jnp.int32))
    return (perm, inverse)


def draw_owner_map(key, part):
    perm, inverse = shared_order(key)
    return perm


def draw_cluster_keys(key, part):
    perm, inverse = shared_order(key)
    key = jax.random.fold_in(key, 12)
    local = jax.random.randint(key, (ROWS,), 0, CLU_DEV, dtype=jnp.int32)
    index = jnp.arange(ROWS, dtype=jnp.int32)
    block = index % ROW_DEV // CAP
    return inverse[block * CLU_DEV + local].astype(jnp.int32)


def draw_live_counts(key, part):
    key = jax.random.fold_in(key, 11)
    first, second, third = jax.random.split(key, 3)
    level = jax.random.randint(first, (N_CLU,), 3, 5, dtype=jnp.int32)
    raw = jax.random.randint(second, (N_CLU * N_ROW, N_CLU), CAP // 2, CAP + 1, dtype=jnp.int32)
    scaled = raw * level[None, :] // 4
    forced = jax.random.randint(third, (N_CLU * N_ROW,), 0, N_CLU, dtype=jnp.int32)
    column = jnp.arange(N_CLU, dtype=jnp.int32)[None, :]
    return jnp.where(column == forced[:, None], CAP, scaled).astype(jnp.int32)


def draw_embeddings(key, part):
    key = jax.random.fold_in(key, 13)
    second = jax.random.fold_in(key, 1)
    values = jnp.clip(jax.random.normal(second, (ROWS, D), jnp.float32), -6.0, 6.0)
    return values.astype(jnp.bfloat16)


def levels(own_key, shape, pieces, smallest, high):
    def one(dim, shards_of):
        heights = jax.random.uniform(jax.random.fold_in(jax.random.fold_in(own_key, 6), dim), (shards_of,), jnp.float32, smallest / len(pieces), high / len(pieces))
        return jnp.repeat(jnp.exp(heights), shape[dim] // shards_of).reshape((-1,) + (1,) * (len(shape) - dim - 1))

    level = one(*pieces[0])
    for cut in pieces[1:]:
        level = level * one(*cut)
    return level


def scatter_about(rng, shape, scale, most, cuts=(), held_as=jnp.bfloat16):
    result = scale * jax.random.normal(rng, shape, jnp.float32)
    if cuts:
        result = result * levels(rng, shape, cuts, -0.22, 0.18)
    return jnp.clip(result, -most, most).astype(held_as)


def setup_inputs(seed: int = 0) -> dict:
    arg_keys = jax.random.split(jax.random.key(seed), 6)
    embeddings = draw_embeddings(jax.random.fold_in(arg_keys[5], 71), 0)
    cluster_keys = draw_cluster_keys(jax.random.fold_in(arg_keys[5], 71), 0)
    owner_map = draw_owner_map(jax.random.fold_in(arg_keys[5], 71), 0)
    live_counts = draw_live_counts(jax.random.fold_in(arg_keys[5], 71), 0)
    sub_centroids = scatter_about(arg_keys[4], (K1, K2, D), 1.0, 6.0, ((0, 32),))
    return dict(embeddings=embeddings, cluster_keys=cluster_keys, owner_map=owner_map, live_counts=live_counts, sub_centroids=sub_centroids)


inverse_temp = 1.0 / 32.0


def owner_update(packed):
    rows, codes, centers = packed
    squares_x = jnp.sum(rows.astype(jnp.float32) ** 2, axis=1)
    squares_c = jnp.sum(centers.astype(jnp.float32) ** 2, axis=1)
    products = jnp.dot(rows, centers.T, preferred_element_type=jnp.float32)
    distance = squares_x[:, None] - 2.0 * products + squares_c[None, :]
    distance = distance.reshape(rows.shape[0], CLU_DEV, K2)
    owned = (codes[:, None] == jnp.arange(CLU_DEV, dtype=jnp.int32)[None, :]).astype(jnp.float32)
    probs = jax.nn.softmax(-distance * inverse_temp, axis=-1) * owned[:, :, None]
    costs = jnp.sum(probs * distance, axis=(1, 2)) / D
    totals = jnp.sum(probs, axis=0).reshape(-1)
    weights = probs.astype(jnp.bfloat16).reshape(rows.shape[0], CLU_DEV * K2)
    sums = jnp.dot(weights.T, rows, preferred_element_type=jnp.float32)
    updated = (sums + centers.astype(jnp.float32)) / (totals[:, None] + 1.0)
    return updated, costs


def reference(embeddings, cluster_keys, owner_map, live_counts, sub_centroids):
    devices_all = N_CLU * N_ROW
    index = jnp.arange(ROWS, dtype=jnp.int32)
    device_of = index // ROW_DEV
    block_of = (index % ROW_DEV) // CAP
    slot_of = index % CAP
    live = slot_of < live_counts[device_of, block_of]
    position = owner_map[cluster_keys]
    codes = jnp.where(live, position % CLU_DEV, -1).astype(jnp.int32)
    rows_by_owner = embeddings.reshape(devices_all, N_CLU, CAP, D).transpose(1, 0, 2, 3).reshape(N_CLU, devices_all * CAP, D)
    codes_by_owner = codes.reshape(devices_all, N_CLU, CAP).transpose(1, 0, 2).reshape(N_CLU, devices_all * CAP)
    centers = sub_centroids.reshape(N_CLU, CLU_DEV * K2, D)
    updated, costs = lax.map(owner_update, (rows_by_owner, codes_by_owner, centers))
    new_centroids = updated.reshape(K1, K2, D)
    row_costs = costs.reshape(N_CLU, devices_all, CAP).transpose(1, 0, 2).reshape(ROWS)
    return new_centroids, row_costs
```

```python
import functools
import jax, jax.numpy as jnp
from jax import lax
from jax.experimental import pallas as pl
from jax.experimental.pallas import tpu as pltpu

inverse_temp = 1.0 / 32.0

def assign_kernel(tile, parts, first, last, *refs):
    it = iter(refs)
    y_ref = next(it) if last else None
    codes_ref, x_ref, c_ref, csq_ref = next(it), next(it), next(it), next(it)
    if not first:
        sums_in, counts_in = next(it), next(it)
    gain_ref = next(it)
    if last:
        own_ref, far = next(it), [next(it), next(it), next(it)]
        side_ref = next(it)
        sums, counts = next(it), next(it)
    else:
        sums, counts = next(it), next(it)
    step = pl.program_id(0)
    centers = c_ref.shape[0]
    clusters = 4
    each = centers // clusters

    @pl.when(step == 0)
    def _():
        if first:
            sums[...] = jnp.zeros_like(sums)
            counts[...] = jnp.zeros_like(counts)
        else:
            sums[...] = sums_in[...]
            counts[...] = counts_in[...]

    sub = tile // parts
    cc = c_ref[...]
    csq = csq_ref[...]
    prods = []
    for p in range(parts):
        prods.append(lax.dot_general(cc, x_ref[p * sub:(p + 1) * sub, :], (((1,), (1,)), ((), ())),
                                     preferred_element_type=jnp.float32))
    for p in range(parts):
        prod = prods[p]
        weights = [[] for _ in range(clusters)]
        tallies = [counts[c * each:(c + 1) * each, :] for c in range(clusters)]
        for j in range(sub // 128):
            lanes = slice(p * sub + j * 128, p * sub + (j + 1) * 128)
            code = codes_ref[0:1, lanes]
            pick = prod[0:each, j * 128:(j + 1) * 128] * (2.0 * inverse_temp) - csq[0:each, :]
            for c in range(1, clusters):
                other = prod[c * each:(c + 1) * each, j * 128:(j + 1) * 128] * (2.0 * inverse_temp) - csq[c * each:(c + 1) * each, :]
                pick = jnp.where(code == c, other, pick)
            top = jnp.max(pick, axis=0, keepdims=True)
            e = jnp.exp(pick - top)
            total = jnp.sum(e, axis=0, keepdims=True)
            inv = 1.0 / total
            gain_ref[0:1, lanes] = jnp.sum(e * pick, axis=0, keepdims=True) * inv * (-1.0 / inverse_temp)
            prob = e * inv
            for c in range(clusters):
                m = jnp.where(code == c, prob, 0.0)
                tallies[c] = tallies[c] + m
                weights[c].append(m.astype(jnp.bfloat16))
        for c in range(clusters):
            counts[c * each:(c + 1) * each, :] = tallies[c]
        w = jnp.concatenate([jnp.concatenate(ws, axis=1) for ws in weights], axis=0)
        sums[...] += jnp.dot(w, x_ref[p * sub:(p + 1) * sub, :], preferred_element_type=jnp.float32)

    if last:
        @pl.when(step == pl.num_programs(0) - 1)
        def _():
            y = y_ref[0]
            quarter = sums.shape[1] // 4
            own_ref[...] = sums[:, pl.ds(pl.multiple_of(y * quarter, quarter), quarter)]
            peak = jnp.max(jnp.abs(sums[...]), axis=1, keepdims=True)
            scale = jnp.maximum(peak, 1e-30) * (1.0 / 32766.0)
            inv = 1.0 / scale
            for k in range(1, 4):
                to = (y + k) % 4
                v = sums[:, pl.ds(pl.multiple_of(to * quarter, quarter), quarter)] * inv
                far[k - 1][...] = jnp.round(v).astype(jnp.int32).astype(jnp.int16)
            tot = jnp.sum(counts[...], axis=1, keepdims=True)
            col = lax.broadcasted_iota(jnp.int32, counts.shape, 1)
            both = jnp.where(col == 0, tot, jnp.where(col == 1, scale, 0.0))
            side_ref[...] = both.T[0:8, :]


def assign(rows, codes, centers, csq, carry=None, y=None, tile=512, parts=2):
    n, d = rows.shape
    m = centers.shape[0]
    first, last = carry is None, y is not None
    f32 = jnp.float32
    whole = lambda shape: pl.BlockSpec(shape, lambda i, *_: (0,) * len(shape))
    in_specs = [pl.BlockSpec((1, tile), lambda i, *_: (0, i)), pl.BlockSpec((tile, d), lambda i, *_: (i, 0)),
                whole((m, d)), whole((m, 1))]
    args = [codes, rows, centers, csq]
    if not first:
        in_specs += [whole((m, d)), whole((m, 128))]
        args += list(carry)
    out_specs = [pl.BlockSpec((1, tile), lambda i, *_: (0, i))]
    outs = [jax.ShapeDtypeStruct((1, n), f32)]
    scratch = []
    if last:
        out_specs += [whole((m, d // 4))] * 4 + [whole((8, m))]
        outs += [jax.ShapeDtypeStruct((m, d // 4), f32)] + [jax.ShapeDtypeStruct((m, d // 4), jnp.int16)] * 3 + [jax.ShapeDtypeStruct((8, m), f32)]
        scratch = [pltpu.VMEM((m, d), f32), pltpu.VMEM((m, 128), f32)]
        args = [y.reshape(1).astype(jnp.int32)] + args
    else:
        out_specs += [whole((m, d)), whole((m, 128))]
        outs += [jax.ShapeDtypeStruct((m, d), f32), jax.ShapeDtypeStruct((m, 128), f32)]
    return pl.pallas_call(
        functools.partial(assign_kernel, tile, parts, first, last),
        grid_spec=pltpu.PrefetchScalarGridSpec(num_scalar_prefetch=1 if last else 0, grid=(n // tile,), in_specs=in_specs,
            out_specs=out_specs, scratch_shapes=scratch),
        out_shape=outs,
        compiler_params=pltpu.CompilerParams(dimension_semantics=("arbitrary",), vmem_limit_bytes=56 * 1024 * 1024),
        cost_estimate=pl.CostEstimate(flops=4 * n * m * d, bytes_accessed=2 * n * d + 2 * m * d + 4 * m * d, transcendentals=n * m // 4),
    )(*args)


from jax.sharding import PartitionSpec as P

cuts = (0, 128)


def around(k, size):
    return [(i, (i + k) % size) for i in range(size)]


def body(embeddings, cluster_keys, owner_map, live_counts, sub_centroids):
    owners = lax.axis_size("clu")
    groups = lax.axis_size("row")
    slots, features = embeddings.shape
    capacity = slots // owners
    clusters_here, centers_each = sub_centroids.shape[:2]
    y = lax.axis_index("row").astype(jnp.int32)

    keys = cluster_keys.reshape(owners, capacity)
    table = jnp.arange(owner_map.shape[0], dtype=jnp.int32)
    position = jnp.sum(jnp.where(keys[:, :, None] == table, owner_map, 0), axis=2)
    live = jnp.arange(capacity, dtype=jnp.int32)[None, :] < live_counts[0][:, None]
    code_blocks = jnp.where(live, position % clusters_here, -1)
    codes_in = lax.all_to_all(code_blocks, "clu", split_axis=0, concat_axis=0, tiled=True)

    blocks = embeddings.reshape(owners, capacity, features)
    received = [
        lax.all_to_all(blocks[:, a:b], "clu", split_axis=0, concat_axis=0, tiled=True)
        for a, b in zip(cuts[:-1], cuts[1:])
    ]
    centers = sub_centroids.reshape(clusters_here * centers_each, features)
    center_squares = jnp.sum(centers.astype(jnp.float32) ** 2, axis=1, keepdims=True) * inverse_temp
    row_squares = jnp.sum(blocks.astype(jnp.float32) ** 2, axis=2)
    share = lax.dynamic_slice_in_dim(centers, y * (features // groups), features // groups, 1)

    carry = None
    gains = []
    for i, (a, b) in enumerate(zip(cuts[:-1], cuts[1:])):
        rows = received[i].reshape(owners * (b - a), features)
        codes = codes_in[:, a:b].reshape(1, owners * (b - a))
        end = b == capacity
        out = assign(rows, codes, centers, center_squares, carry, y if end else None, tiles[i], 2)
        gains.append(out[0].reshape(owners, b - a))
        carry = out[1:]
    own, far1, far2, far3, side = carry

    got2 = lax.ppermute(far2, "row", around(2, groups))
    got1 = lax.ppermute(far1, "row", around(1, groups))
    got3 = lax.ppermute(far3, "row", around(3, groups))
    sides = lax.all_gather(side[0:2], "row")
    returned = lax.all_to_all(jnp.concatenate(gains, axis=1), "clu", split_axis=0, concat_axis=0, tiled=True)

    total = jnp.sum(sides[:, 0], axis=0)
    summed = own + share.astype(jnp.float32)
    for k, got in ((1, got1), (2, got2), (3, got3)):
        scale = lax.dynamic_index_in_dim(sides, (y - k) % groups, 0, keepdims=False)[1]
        summed = summed + got.astype(jnp.float32) * scale[:, None]
    updated = summed / (total[:, None] + 1.0)
    new_centroids = updated.reshape(clusters_here, centers_each, features // groups)
    row_costs = jnp.where(live, row_squares + returned, 0.0) * (1.0 / features)
    return new_centroids, row_costs.reshape(slots)


tiles = (1024,)


def solution(mesh):
    return jax.shard_map(
        body,
        mesh=mesh,
        in_specs=(
            P(("clu", "row"), None),
            P(("clu", "row")),
            P(),
            P(("clu", "row"), None),
            P("clu", None, None),
        ),
        out_specs=(P("clu", None, "row"), P(("clu", "row"))),
        check_vma=False,
    )
```

```python
import functools
import jax, jax.numpy as jnp
from jax import lax
from jax.experimental import pallas as pl
from jax.experimental.pallas import tpu as pltpu

inverse_temp = 1.0 / 32.0
levels = 16.0
most = 32700.0
fine = 32000.0


def step_of(level):
    return jnp.exp2(level * (1.0 / levels)) * (1.0 / most)


def assign_kernel(tile, parts, first, last, *refs):
    it = iter(refs)
    y_ref = next(it) if last else None
    codes_ref, x_ref, c_ref, csq_ref = next(it), next(it), next(it), next(it)
    if not first:
        sums_in, counts_in = next(it), next(it)
    gain_ref = next(it)
    if last:
        own_ref, far = next(it), [next(it), next(it), next(it)]
        home_ref = next(it)
        sums, counts = next(it), next(it)
    else:
        sums, counts = next(it), next(it)
    step = pl.program_id(0)
    centers = c_ref.shape[0]
    clusters = 4
    each = centers // clusters

    @pl.when(step == 0)
    def _():
        if first:
            sums[...] = jnp.zeros_like(sums)
            counts[...] = jnp.zeros_like(counts)
        else:
            sums[...] = sums_in[...]
            counts[...] = counts_in[...]

    sub = tile // parts
    cc = c_ref[...]
    csq = csq_ref[...]
    prods = []
    for p in range(parts):
        prods.append(lax.dot_general(cc, x_ref[p * sub:(p + 1) * sub, :], (((1,), (1,)), ((), ())),
                                     preferred_element_type=jnp.float32))
    for p in range(parts):
        prod = prods[p]
        weights = [[] for _ in range(clusters)]
        tallies = [counts[c * each:(c + 1) * each, :] for c in range(clusters)]
        for j in range(sub // 128):
            lanes = slice(p * sub + j * 128, p * sub + (j + 1) * 128)
            code = codes_ref[0:1, lanes]
            pick = prod[0:each, j * 128:(j + 1) * 128] * (2.0 * inverse_temp) - csq[0:each, :]
            for c in range(1, clusters):
                other = prod[c * each:(c + 1) * each, j * 128:(j + 1) * 128] * (2.0 * inverse_temp) - csq[c * each:(c + 1) * each, :]
                pick = jnp.where(code == c, other, pick)
            top = jnp.max(pick, axis=0, keepdims=True)
            e = jnp.exp(pick - top)
            total = jnp.sum(e, axis=0, keepdims=True)
            inv = 1.0 / total
            gain_ref[0:1, lanes] = jnp.sum(e * pick, axis=0, keepdims=True) * inv * (-1.0 / inverse_temp)
            prob = e * inv
            for c in range(clusters):
                m = jnp.where(code == c, prob, 0.0)
                tallies[c] = tallies[c] + m
                weights[c].append(m.astype(jnp.bfloat16))
        for c in range(clusters):
            counts[c * each:(c + 1) * each, :] = tallies[c]
        w = jnp.concatenate([jnp.concatenate(ws, axis=1) for ws in weights], axis=0)
        sums[...] += jnp.dot(w, x_ref[p * sub:(p + 1) * sub, :], preferred_element_type=jnp.float32)

    if last:
        @pl.when(step == pl.num_programs(0) - 1)
        def _():
            y = y_ref[0]
            quarter = sums.shape[1] // 4
            own_ref[...] = sums[:, pl.ds(pl.multiple_of(y * quarter, quarter), quarter)]
            peak = jnp.max(jnp.abs(sums[...]), axis=1, keepdims=True)
            level = jnp.ceil(jnp.log2(jnp.maximum(peak, 1e-30)) * levels)
            inv = 1.0 / step_of(level)
            for k in range(1, 4):
                to = (y + k) % 4
                v = sums[:, pl.ds(pl.multiple_of(to * quarter, quarter), quarter)] * inv
                far[k - 1][0:centers, :] = jnp.round(v).astype(jnp.int32).astype(jnp.int16)
            tot = jnp.sum(counts[...], axis=1, keepdims=True) * 4.0
            high = jnp.floor(tot)
            low = jnp.round((tot - high) * fine)
            col = lax.broadcasted_iota(jnp.int32, counts.shape, 1)
            notes = jnp.where(col == 0, high, jnp.where(col == 1, low, jnp.where(col == 2, level, 0.0)))
            turned = notes.T[0:16, :].astype(jnp.int32).astype(jnp.int16)
            for g in range(4):
                part = turned[:, g * each:(g + 1) * each]
                home_ref[g * 16:(g + 1) * 16, :] = part
                for k in range(3):
                    far[k][centers + g * 16:centers + (g + 1) * 16, :] = part


def merge_kernel(own_ref, share_ref, home_ref, *refs):
    far, out_ref = refs[:3], refs[3]
    m = own_ref.shape[0]
    each = m // 4
    for g in range(4):
        rows = slice(g * each, (g + 1) * each)
        total = 1.0
        summed = own_ref[rows, :] + share_ref[rows, :].astype(jnp.float32)
        for k in range(4):
            note = far[k - 1][m + g * 16:m + (g + 1) * 16, :] if k else home_ref[g * 16:(g + 1) * 16, :]
            turned = jnp.concatenate([note.astype(jnp.int32).astype(jnp.float32)] * 8, axis=0).T
            total = total + (turned[:, 0:1] + turned[:, 1:2] * (1.0 / fine)) * 0.25
            if k:
                summed = summed + far[k - 1][rows, :].astype(jnp.int32).astype(jnp.float32) * step_of(turned[:, 2:3])
        out_ref[rows, :] = summed / total


def merge(own, share, home, far):
    space = pl.BlockSpec(memory_space=pltpu.VMEM)
    return pl.pallas_call(
        merge_kernel,
        in_specs=[space] * 6,
        out_specs=space,
        out_shape=jax.ShapeDtypeStruct(own.shape, jnp.float32),
        compiler_params=pltpu.CompilerParams(vmem_limit_bytes=24 * 1024 * 1024),
    )(own, share, home, *far)


def assign(rows, codes, centers, csq, carry=None, y=None, tile=512, parts=2):
    n, d = rows.shape
    m = centers.shape[0]
    first, last = carry is None, y is not None
    f32 = jnp.float32
    whole = lambda shape: pl.BlockSpec(shape, lambda i, *_: (0,) * len(shape))
    in_specs = [pl.BlockSpec((1, tile), lambda i, *_: (0, i)), pl.BlockSpec((tile, d), lambda i, *_: (i, 0)),
                whole((m, d)), whole((m, 1))]
    args = [codes, rows, centers, csq]
    if not first:
        in_specs += [whole((m, d)), whole((m, 128))]
        args += list(carry)
    out_specs = [pl.BlockSpec((1, tile), lambda i, *_: (0, i))]
    outs = [jax.ShapeDtypeStruct((1, n), f32)]
    scratch = []
    if last:
        out_specs += [whole((m, d // 4))] + [whole((m + 64, d // 4))] * 3 + [whole((64, d // 4))]
        outs += [jax.ShapeDtypeStruct((m, d // 4), f32)] + [jax.ShapeDtypeStruct((m + 64, d // 4), jnp.int16)] * 3 + [jax.ShapeDtypeStruct((64, d // 4), jnp.int16)]
        scratch = [pltpu.VMEM((m, d), f32), pltpu.VMEM((m, 128), f32)]
        args = [y.reshape(1).astype(jnp.int32)] + args
    else:
        out_specs += [whole((m, d)), whole((m, 128))]
        outs += [jax.ShapeDtypeStruct((m, d), f32), jax.ShapeDtypeStruct((m, 128), f32)]
    return pl.pallas_call(
        functools.partial(assign_kernel, tile, parts, first, last),
        grid_spec=pltpu.PrefetchScalarGridSpec(num_scalar_prefetch=1 if last else 0, grid=(n // tile,), in_specs=in_specs,
            out_specs=out_specs, scratch_shapes=scratch),
        out_shape=outs,
        compiler_params=pltpu.CompilerParams(dimension_semantics=("arbitrary",), vmem_limit_bytes=56 * 1024 * 1024),
        cost_estimate=pl.CostEstimate(flops=4 * n * m * d, bytes_accessed=2 * n * d + 2 * m * d + 4 * m * d, transcendentals=n * m // 4),
    )(*args)


from jax.sharding import PartitionSpec as P

cuts = (0, 128)


def around(k, size):
    return [(i, (i + k) % size) for i in range(size)]


def body(embeddings, cluster_keys, owner_map, live_counts, sub_centroids):
    owners = lax.axis_size("clu")
    groups = lax.axis_size("row")
    slots, features = embeddings.shape
    capacity = slots // owners
    clusters_here, centers_each = sub_centroids.shape[:2]
    y = lax.axis_index("row").astype(jnp.int32)

    keys = cluster_keys.reshape(owners, capacity)
    table = jnp.arange(owner_map.shape[0], dtype=jnp.int32)
    position = jnp.sum(jnp.where(keys[:, :, None] == table, owner_map, 0), axis=2)
    live = jnp.arange(capacity, dtype=jnp.int32)[None, :] < live_counts[0][:, None]
    code_blocks = jnp.where(live, position % clusters_here, -1)
    gathered = lax.all_gather(code_blocks.astype(jnp.int16), "clu")
    me = lax.axis_index("clu")
    codes_in = lax.dynamic_index_in_dim(gathered, me, 1, keepdims=False).astype(jnp.int32)

    blocks = embeddings.reshape(owners, capacity, features)
    received = [
        lax.all_to_all(blocks[:, a:b], "clu", split_axis=0, concat_axis=0, tiled=True)
        for a, b in zip(cuts[:-1], cuts[1:])
    ]
    centers = sub_centroids.reshape(clusters_here * centers_each, features)
    center_squares = jnp.sum(centers.astype(jnp.float32) ** 2, axis=1, keepdims=True) * inverse_temp
    row_squares = jnp.sum(blocks.astype(jnp.float32) ** 2, axis=2)

    share = lax.dynamic_slice_in_dim(centers, y * (features // groups), features // groups, 1)
    carry = None
    gains = []
    for i, (a, b) in enumerate(zip(cuts[:-1], cuts[1:])):
        rows = received[i].reshape(owners * (b - a), features)
        codes = codes_in[:, a:b].reshape(1, owners * (b - a))
        end = b == capacity
        out = assign(rows, codes, centers, center_squares, carry, y if end else None, tiles[i], 2)
        gains.append(out[0].reshape(owners, b - a))
        carry = out[1:]
    own, far1, far2, far3, home = carry

    got2 = lax.ppermute(far2, "row", around(2, groups))
    got1 = lax.ppermute(far1, "row", around(1, groups))
    got3 = lax.ppermute(far3, "row", around(3, groups))
    returned = lax.all_to_all(jnp.concatenate(gains, axis=1), "clu", split_axis=0, concat_axis=0, tiled=True)
    updated = merge(own, share, home, (got1, got2, got3))
    new_centroids = updated.reshape(clusters_here, centers_each, features // groups)
    row_costs = jnp.where(live, row_squares + returned, 0.0) * (1.0 / features)
    return new_centroids, row_costs.reshape(slots)


tiles = (1024,)


def solution(mesh):
    return jax.shard_map(
        body,
        mesh=mesh,
        in_specs=(
            P(("clu", "row"), None),
            P(("clu", "row")),
            P(),
            P(("clu", "row"), None),
            P("clu", None, None),
        ),
        out_specs=(P("clu", None, "row"), P(("clu", "row"))),
        check_vma=False,
    )
```

```python
import functools
import jax, jax.numpy as jnp
from jax import lax
from jax.experimental import pallas as pl
from jax.experimental.pallas import tpu as pltpu

inverse_temp = 1.0 / 32.0
levels = 16.0
most = 32700.0
fine = 32000.0


def step_of(level):
    return jnp.exp2(level * (1.0 / levels)) * (1.0 / most)


def assign_kernel(tile, parts, first, last, *refs):
    it = iter(refs)
    y_ref = next(it) if last else None
    codes_ref, x_ref, c_ref, csq_ref = next(it), next(it), next(it), next(it)
    if not first:
        sums_in, counts_in = next(it), next(it)
    gain_ref = next(it)
    if last:
        own_ref, far = next(it), [next(it), next(it), next(it)]
        home_ref = next(it)
        sums, counts, arrived = next(it), next(it), next(it)
    else:
        sums, counts = next(it), next(it)
    step = pl.program_id(0)
    centers = c_ref.shape[0]
    clusters = 4
    each = centers // clusters

    @pl.when(step == 0)
    def _():
        if first:
            sums[...] = jnp.zeros_like(sums)
            counts[...] = jnp.zeros_like(counts)
        else:
            pltpu.make_async_copy(sums_in, sums, arrived.at[0]).start()
            pltpu.make_async_copy(counts_in, counts, arrived.at[1]).start()

    sub = tile // parts
    cc = c_ref[...]
    csq = csq_ref[...]
    prods = []
    for p in range(parts):
        prods.append(lax.dot_general(cc, x_ref[p * sub:(p + 1) * sub, :], (((1,), (1,)), ((), ())),
                                     preferred_element_type=jnp.float32))
    if not first:
        @pl.when(step == 0)
        def _():
            pltpu.make_async_copy(counts_in, counts, arrived.at[1]).wait()
            pltpu.make_async_copy(sums_in, sums, arrived.at[0]).wait()

    for p in range(parts):
        prod = prods[p]
        weights = [[] for _ in range(clusters)]
        tallies = [counts[c * each:(c + 1) * each, :] for c in range(clusters)]
        for j in range(sub // 128):
            lanes = slice(p * sub + j * 128, p * sub + (j + 1) * 128)
            code = codes_ref[0:1, lanes]
            pick = prod[0:each, j * 128:(j + 1) * 128] * (2.0 * inverse_temp) - csq[0:each, :]
            for c in range(1, clusters):
                other = prod[c * each:(c + 1) * each, j * 128:(j + 1) * 128] * (2.0 * inverse_temp) - csq[c * each:(c + 1) * each, :]
                pick = jnp.where(code == c, other, pick)
            top = jnp.max(pick, axis=0, keepdims=True)
            e = jnp.exp(pick - top)
            total = jnp.sum(e, axis=0, keepdims=True)
            inv = 1.0 / total
            gain_ref[0:1, lanes] = jnp.sum(e * pick, axis=0, keepdims=True) * inv * (-1.0 / inverse_temp)
            prob = e * inv
            for c in range(clusters):
                m = jnp.where(code == c, prob, 0.0)
                tallies[c] = tallies[c] + m
                weights[c].append(m.astype(jnp.bfloat16))
        for c in range(clusters):
            counts[c * each:(c + 1) * each, :] = tallies[c]
        w = jnp.concatenate([jnp.concatenate(ws, axis=1) for ws in weights], axis=0)
        sums[...] += jnp.dot(w, x_ref[p * sub:(p + 1) * sub, :], preferred_element_type=jnp.float32)

    if last:
        @pl.when(step == pl.num_programs(0) - 1)
        def _():
            y = y_ref[0]
            quarter = sums.shape[1] // 4
            own_ref[...] = sums[:, pl.ds(pl.multiple_of(y * quarter, quarter), quarter)]
            peak = jnp.max(jnp.abs(sums[...]), axis=1, keepdims=True)
            level = jnp.ceil(jnp.log2(jnp.maximum(peak, 1e-30)) * levels)
            inv = 1.0 / step_of(level)
            for k in range(1, 4):
                to = (y + k) % 4
                v = sums[:, pl.ds(pl.multiple_of(to * quarter, quarter), quarter)] * inv
                far[k - 1][0:centers, :] = jnp.round(v).astype(jnp.int32).astype(jnp.int16)
            tot = jnp.sum(counts[...], axis=1, keepdims=True) * 4.0
            high = jnp.floor(tot)
            low = jnp.round((tot - high) * fine)
            col = lax.broadcasted_iota(jnp.int32, counts.shape, 1)
            notes = jnp.where(col == 0, high, jnp.where(col == 1, low, jnp.where(col == 2, level, 0.0)))
            turned = notes.T[0:16, :].astype(jnp.int32).astype(jnp.int16)
            for g in range(4):
                part = turned[:, g * each:(g + 1) * each]
                home_ref[g * 16:(g + 1) * 16, :] = part
                for k in range(3):
                    far[k][centers + g * 16:centers + (g + 1) * 16, :] = part


def merge_kernel(own_ref, share_ref, home_ref, *refs):
    far, out_ref = refs[:3], refs[3]
    each = own_ref.shape[0]
    m = 4 * each
    g = pl.program_id(0)
    rows = pl.ds(pl.multiple_of(g * each, each), each)
    marks = pl.ds(pl.multiple_of(m + g * 16, 16), 16)
    total = 1.0
    summed = own_ref[...] + share_ref[...].astype(jnp.float32)
    for k in range(4):
        note = far[k - 1][marks, :] if k else home_ref[...]
        turned = jnp.concatenate([note.astype(jnp.int32).astype(jnp.float32)] * 8, axis=0).T
        total = total + (turned[:, 0:1] + turned[:, 1:2] * (1.0 / fine)) * 0.25
        if k:
            summed = summed + far[k - 1][rows, :].astype(jnp.int32).astype(jnp.float32) * step_of(turned[:, 2:3])
    out_ref[...] = summed / total


def merge(own, share, home, far):
    m, quarter = own.shape
    block = pl.BlockSpec((m // 4, quarter), lambda i: (i, 0))
    return pl.pallas_call(
        merge_kernel,
        grid=(4,),
        in_specs=[block, block, pl.BlockSpec((16, quarter), lambda i: (i, 0))] + [pl.BlockSpec(memory_space=pltpu.VMEM)] * 3,
        out_specs=block,
        out_shape=jax.ShapeDtypeStruct(own.shape, jnp.float32),
        compiler_params=pltpu.CompilerParams(dimension_semantics=("arbitrary",), vmem_limit_bytes=24 * 1024 * 1024),
    )(own, share, home, *far)


def pack_kernel(clusters, cut, keys_ref, map_ref, used_ref, x_ref, out_ref):
    owners, capacity = keys_ref.shape
    first = owners * pl.program_id(0)
    table = jnp.broadcast_to(map_ref[...], (owners, capacity))
    position = jnp.take_along_axis(table, keys_ref[...], axis=1)
    used = jnp.broadcast_to(used_ref[...], (owners, used_ref.shape[1]))
    mine = lax.broadcasted_iota(jnp.int32, used.shape, 1) == first + lax.broadcasted_iota(jnp.int32, used.shape, 0)
    limit = jnp.sum(jnp.where(mine, used, 0), axis=1, keepdims=True)
    live = lax.broadcasted_iota(jnp.int32, position.shape, 1) < limit
    codes = jnp.where(live, lax.rem(position, clusters), -1)
    edge = out_ref.shape[1] - 16
    out_ref[:, 0:edge, :] = x_ref[:, 0:edge, :]
    high = codes.astype(jnp.float32)
    wide = jnp.concatenate([high] * (x_ref.shape[2] // capacity), axis=1)
    row = lax.broadcasted_iota(jnp.int32, (16, x_ref.shape[2]), 0) + edge
    for j in range(owners):
        kept = x_ref[j, edge:edge + 16, :].astype(jnp.float32)
        out_ref[j, edge:edge + 16, :] = jnp.where(row < cut, kept, wide[j:j + 1, :]).astype(jnp.bfloat16)


def pack(blocks, keys, owner_map, used, clusters, cut, rows):
    owners, capacity, features = blocks.shape
    group = 8
    return pl.pallas_call(
        functools.partial(pack_kernel, clusters, cut),
        grid=(owners // group,),
        in_specs=[
            pl.BlockSpec((group, capacity), lambda i: (i, 0)),
            pl.BlockSpec((1, owner_map.shape[0]), lambda i: (0, 0)),
            pl.BlockSpec((1, owners), lambda i: (0, 0)),
            pl.BlockSpec((group, rows, features), lambda i: (i, 0, 0)),
        ],
        out_specs=pl.BlockSpec((group, rows, features), lambda i: (i, 0, 0)),
        out_shape=jax.ShapeDtypeStruct((owners, rows, features), blocks.dtype),
        compiler_params=pltpu.CompilerParams(dimension_semantics=("arbitrary",)),
    )(keys, owner_map.reshape(1, -1), used, blocks)


def assign(rows, codes, centers, csq, carry=None, y=None, tile=512, parts=2):
    n, d = rows.shape
    m = centers.shape[0]
    first, last = carry is None, y is not None
    f32 = jnp.float32
    resident = pl.BlockSpec(memory_space=pltpu.VMEM)
    whole = lambda shape: pl.BlockSpec(shape, lambda i, *_: (0,) * len(shape))
    in_specs = [pl.BlockSpec((1, tile), lambda i, *_: (0, i)), pl.BlockSpec((tile, d), lambda i, *_: (i, 0)),
                resident, resident]
    args = [codes, rows, centers, csq]
    if not first:
        in_specs += [pl.BlockSpec(memory_space=pl.ANY)] * 2
        args += list(carry)
    out_specs = [pl.BlockSpec((1, tile), lambda i, *_: (0, i))]
    outs = [jax.ShapeDtypeStruct((1, n), f32)]
    scratch = []
    if last:
        out_specs += [whole((m, d // 4))] + [whole((m + 64, d // 4))] * 3 + [whole((64, d // 4))]
        outs += [jax.ShapeDtypeStruct((m, d // 4), f32)] + [jax.ShapeDtypeStruct((m + 64, d // 4), jnp.int16)] * 3 + [jax.ShapeDtypeStruct((64, d // 4), jnp.int16)]
        scratch = [pltpu.VMEM((m, d), f32), pltpu.VMEM((m, 128), f32), pltpu.SemaphoreType.DMA((2,))]
        args = [y.reshape(1).astype(jnp.int32)] + args
    else:
        out_specs += [whole((m, d)), whole((m, 128))]
        outs += [jax.ShapeDtypeStruct((m, d), f32), jax.ShapeDtypeStruct((m, 128), f32)]
    return pl.pallas_call(
        functools.partial(assign_kernel, tile, parts, first, last),
        grid_spec=pltpu.PrefetchScalarGridSpec(num_scalar_prefetch=1 if last else 0, grid=(n // tile,), in_specs=in_specs,
            out_specs=out_specs, scratch_shapes=scratch),
        out_shape=outs,
        compiler_params=pltpu.CompilerParams(dimension_semantics=("arbitrary",), vmem_limit_bytes=60 * 1024 * 1024),
        cost_estimate=pl.CostEstimate(flops=4 * n * m * d, bytes_accessed=2 * n * d + 2 * m * d + 4 * m * d, transcendentals=n * m // 4),
    )(*args)


from jax.sharding import PartitionSpec as P

cut, extra = 88, 8
tiles = (1024, 1280)
parts = (2, 2)


def around(k, size):
    return [(i, (i + k) % size) for i in range(size)]


def body(embeddings, cluster_keys, owner_map, live_counts, sub_centroids):
    owners = lax.axis_size("clu")
    groups = lax.axis_size("row")
    slots, features = embeddings.shape
    capacity = slots // owners
    clusters_here, centers_each = sub_centroids.shape[:2]
    y = lax.axis_index("row").astype(jnp.int32)

    keys = cluster_keys.reshape(owners, capacity)
    blocks = embeddings.reshape(owners, capacity, features)
    centers = sub_centroids.reshape(clusters_here * centers_each, features)
    center_squares = jnp.sum(centers.astype(jnp.float32) ** 2, axis=1, keepdims=True) * inverse_temp
    row_squares = jnp.sum(blocks.astype(jnp.float32) ** 2, axis=2)
    share = lax.dynamic_slice_in_dim(centers, y * (features // groups), features // groups, 1)

    first = pack(blocks, keys, owner_map, live_counts, clusters_here, cut, cut + extra)
    second = blocks[:, cut:]
    second, center_squares, row_squares, share = lax.optimization_barrier(
        (second, center_squares, row_squares, share)
    )
    received = [
        lax.all_to_all(part, "clu", split_axis=0, concat_axis=0, tiled=True)
        for part in (first, second)
    ]
    codes_in = received[0][:, cut, :capacity].astype(jnp.int32)
    none = jnp.full((owners, extra), -1, jnp.int32)
    codes = (jnp.concatenate([codes_in[:, :cut], none], axis=1), codes_in[:, cut:])
    carry = None
    gains = []
    for i in range(2):
        count = received[i].shape[1]
        rows = received[i].reshape(owners * count, features)
        out = assign(rows, codes[i].reshape(1, owners * count), centers, center_squares, carry, y if i else None, tiles[i], parts[i])
        gains.append(out[0].reshape(owners, count))
        carry = out[1:]
    gains[0] = gains[0][:, :cut]
    own, far1, far2, far3, home = carry

    got2 = lax.ppermute(far2, "row", around(2, groups))
    got1 = lax.ppermute(far1, "row", around(1, groups))
    got3 = lax.ppermute(far3, "row", around(3, groups))
    returned = lax.all_to_all(jnp.concatenate(gains, axis=1), "clu", split_axis=0, concat_axis=0, tiled=True)
    updated = merge(own, share, home, (got1, got2, got3))
    new_centroids = updated.reshape(clusters_here, centers_each, features // groups)
    live = jnp.arange(capacity, dtype=jnp.int32)[None, :] < live_counts[0][:, None]
    row_costs = jnp.where(live, row_squares + returned, 0.0) * (1.0 / features)
    return new_centroids, row_costs.reshape(slots)


def solution(mesh):
    return jax.shard_map(
        body,
        mesh=mesh,
        in_specs=(
            P(("clu", "row"), None),
            P(("clu", "row")),
            P(),
            P(("clu", "row"), None),
            P("clu", None, None),
        ),
        out_specs=(P("clu", None, "row"), P(("clu", "row"))),
        check_vma=False,
    )
```

```python
import functools
import jax, jax.numpy as jnp
from jax import lax
from jax.experimental import pallas as pl
from jax.experimental.pallas import tpu as pltpu

inverse_temp = 1.0 / 32.0
levels = 16.0
most = 32700.0
fine = 32000.0


def step_of(level):
    return jnp.exp2(level * (1.0 / levels)) * (1.0 / most)


def assign_kernel(tile, parts, first, last, *refs):
    it = iter(refs)
    y_ref = next(it) if last else None
    codes_ref, x_ref, c_ref, csq_ref = next(it), next(it), next(it), next(it)
    if not first:
        sums_in, counts_in = next(it), next(it)
    gain_ref = next(it)
    if last:
        own_ref, far = next(it), [next(it), next(it), next(it)]
        home_ref = next(it)
        sums, counts, arrived = next(it), next(it), next(it)
    else:
        sums, counts = next(it), next(it)
    step = pl.program_id(0)
    centers = c_ref.shape[0]
    clusters = 4
    each = centers // clusters

    @pl.when(step == 0)
    def _():
        if first:
            sums[...] = jnp.zeros_like(sums)
            counts[...] = jnp.zeros_like(counts)
        else:
            pltpu.make_async_copy(sums_in, sums, arrived.at[0]).start()
            pltpu.make_async_copy(counts_in, counts, arrived.at[1]).start()

    sub = tile // parts
    cc = c_ref[...]
    csq = csq_ref[...]
    prods = []
    for p in range(parts):
        prods.append(lax.dot_general(cc, x_ref[p * sub:(p + 1) * sub, :], (((1,), (1,)), ((), ())),
                                     preferred_element_type=jnp.float32))
    if not first:
        @pl.when(step == 0)
        def _():
            pltpu.make_async_copy(counts_in, counts, arrived.at[1]).wait()
            pltpu.make_async_copy(sums_in, sums, arrived.at[0]).wait()

    for p in range(parts):
        prod = prods[p]
        weights = [[] for _ in range(clusters)]
        tallies = [counts[c * each:(c + 1) * each, :] for c in range(clusters)]
        for j in range(sub // 128):
            lanes = slice(p * sub + j * 128, p * sub + (j + 1) * 128)
            code = codes_ref[0:1, lanes]
            pick = prod[0:each, j * 128:(j + 1) * 128] * (2.0 * inverse_temp) - csq[0:each, :]
            for c in range(1, clusters):
                other = prod[c * each:(c + 1) * each, j * 128:(j + 1) * 128] * (2.0 * inverse_temp) - csq[c * each:(c + 1) * each, :]
                pick = jnp.where(code == c, other, pick)
            top = jnp.max(pick, axis=0, keepdims=True)
            e = jnp.exp(pick - top)
            total = jnp.sum(e, axis=0, keepdims=True)
            inv = 1.0 / total
            gain_ref[0:1, lanes] = jnp.sum(e * pick, axis=0, keepdims=True) * inv * (-1.0 / inverse_temp)
            prob = e * inv
            for c in range(clusters):
                m = jnp.where(code == c, prob, 0.0)
                tallies[c] = tallies[c] + m
                weights[c].append(m.astype(jnp.bfloat16))
        for c in range(clusters):
            counts[c * each:(c + 1) * each, :] = tallies[c]
        w = jnp.concatenate([jnp.concatenate(ws, axis=1) for ws in weights], axis=0)
        sums[...] += jnp.dot(w, x_ref[p * sub:(p + 1) * sub, :], preferred_element_type=jnp.float32)

    if last:
        @pl.when(step == pl.num_programs(0) - 1)
        def _():
            y = y_ref[0]
            quarter = sums.shape[1] // 4
            own_ref[...] = sums[:, pl.ds(pl.multiple_of(y * quarter, quarter), quarter)]
            peak = jnp.max(jnp.abs(sums[...]), axis=1, keepdims=True)
            level = jnp.ceil(jnp.log2(jnp.maximum(peak, 1e-30)) * levels)
            inv = 1.0 / step_of(level)
            for k in range(1, 4):
                to = (y + k) % 4
                v = sums[:, pl.ds(pl.multiple_of(to * quarter, quarter), quarter)] * inv
                far[k - 1][0:centers, :] = jnp.round(v).astype(jnp.int32).astype(jnp.int16)
            tot = jnp.sum(counts[...], axis=1, keepdims=True) * 4.0
            high = jnp.floor(tot)
            low = jnp.round((tot - high) * fine)
            col = lax.broadcasted_iota(jnp.int32, counts.shape, 1)
            notes = jnp.where(col == 0, high, jnp.where(col == 1, low, jnp.where(col == 2, level, 0.0)))
            turned = notes.T[0:16, :].astype(jnp.int32).astype(jnp.int16)
            for g in range(4):
                part = turned[:, g * each:(g + 1) * each]
                home_ref[g * 16:(g + 1) * 16, :] = part
                for k in range(3):
                    far[k][centers + g * 16:centers + (g + 1) * 16, :] = part


def merge_kernel(own_ref, home_ref, *refs):
    far, out_ref = refs[:3], refs[3]
    each = own_ref.shape[0]
    m = 4 * each
    g = pl.program_id(0)
    rows = pl.ds(pl.multiple_of(g * each, each), each)
    marks = pl.ds(pl.multiple_of(m + g * 16, 16), 16)
    total = 1.0
    summed = own_ref[...]
    for k in range(4):
        note = far[k - 1][marks, :].astype(jnp.int32).astype(jnp.float32) if k else home_ref[...]
        turned = jnp.concatenate([note] * 8, axis=0).T
        total = total + (turned[:, 0:1] + turned[:, 1:2] * (1.0 / fine)) * 0.25
        if k:
            summed = summed + far[k - 1][rows, :].astype(jnp.int32).astype(jnp.float32) * step_of(turned[:, 2:3])
    out_ref[...] = summed / total


def merge(own, home, far):
    m, quarter = own.shape
    block = pl.BlockSpec((m // 4, quarter), lambda i: (i, 0))
    return pl.pallas_call(
        merge_kernel,
        grid=(4,),
        in_specs=[block, pl.BlockSpec((16, quarter), lambda i: (i, 0))] + [pl.BlockSpec(memory_space=pltpu.VMEM)] * 3,
        out_specs=block,
        out_shape=jax.ShapeDtypeStruct(own.shape, jnp.float32),
        compiler_params=pltpu.CompilerParams(dimension_semantics=("arbitrary",), vmem_limit_bytes=24 * 1024 * 1024),
    )(own, home, *far)


def pack_kernel(clusters, cut, keys_ref, map_ref, used_ref, x_ref, out_ref):
    owners, capacity = keys_ref.shape
    first = owners * pl.program_id(0)
    table = jnp.broadcast_to(map_ref[...], (owners, capacity))
    position = jnp.take_along_axis(table, keys_ref[...], axis=1)
    used = jnp.broadcast_to(used_ref[...], (owners, used_ref.shape[1]))
    mine = lax.broadcasted_iota(jnp.int32, used.shape, 1) == first + lax.broadcasted_iota(jnp.int32, used.shape, 0)
    limit = jnp.sum(jnp.where(mine, used, 0), axis=1, keepdims=True)
    live = lax.broadcasted_iota(jnp.int32, position.shape, 1) < limit
    codes = jnp.where(live, lax.rem(position, clusters), -1)
    edge = out_ref.shape[1] - 16
    out_ref[:, 0:edge, :] = x_ref[:, 0:edge, :]
    high = codes.astype(jnp.float32)
    wide = jnp.concatenate([high] * (x_ref.shape[2] // capacity), axis=1)
    row = lax.broadcasted_iota(jnp.int32, (16, x_ref.shape[2]), 0) + edge
    for j in range(owners):
        kept = x_ref[j, edge:edge + 16, :].astype(jnp.float32)
        out_ref[j, edge:edge + 16, :] = jnp.where(row < cut, kept, wide[j:j + 1, :]).astype(jnp.bfloat16)


def pack(blocks, keys, owner_map, used, clusters, cut, rows):
    owners, capacity, features = blocks.shape
    group = 8
    return pl.pallas_call(
        functools.partial(pack_kernel, clusters, cut),
        grid=(owners // group,),
        in_specs=[
            pl.BlockSpec((group, capacity), lambda i: (i, 0)),
            pl.BlockSpec((1, owner_map.shape[0]), lambda i: (0, 0)),
            pl.BlockSpec((1, owners), lambda i: (0, 0)),
            pl.BlockSpec((group, rows, features), lambda i: (i, 0, 0)),
        ],
        out_specs=pl.BlockSpec((group, rows, features), lambda i: (i, 0, 0)),
        out_shape=jax.ShapeDtypeStruct((owners, rows, features), blocks.dtype),
        compiler_params=pltpu.CompilerParams(dimension_semantics=("arbitrary",)),
    )(keys, owner_map.reshape(1, -1), used, blocks)


def assign(rows, codes, centers, csq, carry=None, y=None, tile=512, parts=2):
    n, d = rows.shape
    m = centers.shape[0]
    first, last = carry is None, y is not None
    f32 = jnp.float32
    resident = pl.BlockSpec(memory_space=pltpu.VMEM)
    whole = lambda shape: pl.BlockSpec(shape, lambda i, *_: (0,) * len(shape))
    in_specs = [pl.BlockSpec((1, tile), lambda i, *_: (0, i)), pl.BlockSpec((tile, d), lambda i, *_: (i, 0)),
                resident, resident]
    args = [codes, rows, centers, csq]
    if not first:
        in_specs += [pl.BlockSpec(memory_space=pl.ANY)] * 2
        args += list(carry)
    out_specs = [pl.BlockSpec((1, tile), lambda i, *_: (0, i))]
    outs = [jax.ShapeDtypeStruct((1, n), f32)]
    scratch = []
    if last:
        out_specs += [whole((m, d // 4))] + [whole((m + 64, d // 4))] * 3 + [whole((64, d // 4))]
        outs += [jax.ShapeDtypeStruct((m, d // 4), f32)] + [jax.ShapeDtypeStruct((m + 64, d // 4), jnp.int16)] * 3 + [jax.ShapeDtypeStruct((64, d // 4), jnp.int16)]
        scratch = [pltpu.VMEM((m, d), f32), pltpu.VMEM((m, 128), f32), pltpu.SemaphoreType.DMA((2,))]
        args = [y.reshape(1).astype(jnp.int32)] + args
    else:
        out_specs += [whole((m, d)), whole((m, 128))]
        outs += [jax.ShapeDtypeStruct((m, d), f32), jax.ShapeDtypeStruct((m, 128), f32)]
    return pl.pallas_call(
        functools.partial(assign_kernel, tile, parts, first, last),
        grid_spec=pltpu.PrefetchScalarGridSpec(num_scalar_prefetch=1 if last else 0, grid=(n // tile,), in_specs=in_specs,
            out_specs=out_specs, scratch_shapes=scratch),
        out_shape=outs,
        compiler_params=pltpu.CompilerParams(dimension_semantics=("arbitrary",), vmem_limit_bytes=60 * 1024 * 1024),
        cost_estimate=pl.CostEstimate(flops=4 * n * m * d, bytes_accessed=2 * n * d + 2 * m * d + 4 * m * d, transcendentals=n * m // 4),
    )(*args)


from jax.sharding import PartitionSpec as P

cut, extra = 88, 8
tiles = (1024, 1280)
parts = (2, 1)


def around(k, size):
    return [(i, (i + k) % size) for i in range(size)]


def body(embeddings, cluster_keys, owner_map, live_counts, sub_centroids):
    owners = lax.axis_size("clu")
    groups = lax.axis_size("row")
    slots, features = embeddings.shape
    capacity = slots // owners
    clusters_here, centers_each = sub_centroids.shape[:2]
    y = lax.axis_index("row").astype(jnp.int32)

    keys = cluster_keys.reshape(owners, capacity)
    blocks = embeddings.reshape(owners, capacity, features)
    centers = sub_centroids.reshape(clusters_here * centers_each, features)
    center_squares = jnp.sum(centers.astype(jnp.float32) ** 2, axis=1, keepdims=True) * inverse_temp
    row_squares = jnp.sum(blocks.astype(jnp.float32) ** 2, axis=2)
    share = lax.dynamic_slice_in_dim(centers, y * (features // groups), features // groups, 1)

    first = pack(blocks, keys, owner_map, live_counts, clusters_here, cut, cut + extra)
    second = blocks[:, cut:]
    second, center_squares, row_squares, share = lax.optimization_barrier(
        (second, center_squares, row_squares, share)
    )
    received = [
        lax.all_to_all(part, "clu", split_axis=0, concat_axis=0, tiled=True)
        for part in (first, second)
    ]
    codes_in = received[0][:, cut, :capacity].astype(jnp.int32)
    none = jnp.full((owners, extra), -1, jnp.int32)
    codes = (jnp.concatenate([codes_in[:, :cut], none], axis=1), codes_in[:, cut:])
    carry = None
    gains = []
    for i in range(2):
        count = received[i].shape[1]
        rows = received[i].reshape(owners * count, features)
        out = assign(rows, codes[i].reshape(1, owners * count), centers, center_squares, carry, y if i else None, tiles[i], parts[i])
        gains.append(out[0].reshape(owners, count))
        carry = out[1:]
    gains[0] = gains[0][:, :cut]
    own, far1, far2, far3, home = carry

    got2 = lax.ppermute(far2, "row", around(2, groups))
    got1 = lax.ppermute(far1, "row", around(1, groups))
    got3 = lax.ppermute(far3, "row", around(3, groups))
    returned = lax.all_to_all(jnp.concatenate(gains, axis=1), "clu", split_axis=0, concat_axis=0, tiled=True)
    updated = merge(own + share.astype(jnp.float32), home.astype(jnp.float32), (got1, got2, got3))
    new_centroids = updated.reshape(clusters_here, centers_each, features // groups)
    live = jnp.arange(capacity, dtype=jnp.int32)[None, :] < live_counts[0][:, None]
    row_costs = jnp.where(live, row_squares + returned, 0.0) * (1.0 / features)
    return new_centroids, row_costs.reshape(slots)


def solution(mesh):
    return jax.shard_map(
        body,
        mesh=mesh,
        in_specs=(
            P(("clu", "row"), None),
            P(("clu", "row")),
            P(),
            P(("clu", "row"), None),
            P("clu", None, None),
        ),
        out_specs=(P("clu", None, "row"), P(("clu", "row"))),
        check_vma=False,
    )
```

```python
import functools
import jax, jax.numpy as jnp
from jax import lax
from jax.experimental import pallas as pl
from jax.experimental.pallas import tpu as pltpu

inverse_temp = 1.0 / 32.0
levels = 16.0
most = 32700.0
fine = 32000.0


def step_of(level):
    return jnp.exp2(level * (1.0 / levels)) * (1.0 / most)


def assign_kernel(tile, parts, first, last, *refs):
    it = iter(refs)
    y_ref = next(it) if last else None
    codes_ref, x_ref, c_ref, csq_ref = next(it), next(it), next(it), next(it)
    if not first:
        sums_in, counts_in = next(it), next(it)
    gain_ref = next(it)
    if last:
        own_ref, far = next(it), [next(it), next(it), next(it)]
        home_ref = next(it)
        sums, counts, arrived = next(it), next(it), next(it)
    else:
        sums, counts = next(it), next(it)
    step = pl.program_id(0)
    centers = c_ref.shape[0]
    clusters = 4
    each = centers // clusters

    @pl.when(step == 0)
    def _():
        if first:
            sums[...] = jnp.zeros_like(sums)
            counts[...] = jnp.zeros_like(counts)
        else:
            pltpu.make_async_copy(sums_in, sums, arrived.at[0]).start()
            pltpu.make_async_copy(counts_in, counts, arrived.at[1]).start()

    sub = tile // parts
    cc = c_ref[...]
    csq = csq_ref[...]
    prods = []
    for p in range(parts):
        prods.append(lax.dot_general(cc, x_ref[p * sub:(p + 1) * sub, :], (((1,), (1,)), ((), ())),
                                     preferred_element_type=jnp.float32))
    if not first:
        @pl.when(step == 0)
        def _():
            pltpu.make_async_copy(counts_in, counts, arrived.at[1]).wait()
            pltpu.make_async_copy(sums_in, sums, arrived.at[0]).wait()

    for p in range(parts):
        prod = prods[p]
        weights = [[] for _ in range(clusters)]
        tallies = [counts[c * each:(c + 1) * each, :] for c in range(clusters)]
        for j in range(sub // 128):
            lanes = slice(p * sub + j * 128, p * sub + (j + 1) * 128)
            code = codes_ref[0:1, lanes]
            pick = prod[0:each, j * 128:(j + 1) * 128] * (2.0 * inverse_temp) - csq[0:each, :]
            for c in range(1, clusters):
                other = prod[c * each:(c + 1) * each, j * 128:(j + 1) * 128] * (2.0 * inverse_temp) - csq[c * each:(c + 1) * each, :]
                pick = jnp.where(code == c, other, pick)
            top = jnp.max(pick, axis=0, keepdims=True)
            e = jnp.exp(pick - top)
            total = jnp.sum(e, axis=0, keepdims=True)
            inv = 1.0 / total
            gain_ref[0:1, lanes] = jnp.sum(e * pick, axis=0, keepdims=True) * inv * (-1.0 / inverse_temp)
            prob = e * inv
            for c in range(clusters):
                m = jnp.where(code == c, prob, 0.0)
                tallies[c] = tallies[c] + m
                weights[c].append(m.astype(jnp.bfloat16))
        for c in range(clusters):
            counts[c * each:(c + 1) * each, :] = tallies[c]
        w = jnp.concatenate([jnp.concatenate(ws, axis=1) for ws in weights], axis=0)
        sums[...] += jnp.dot(w, x_ref[p * sub:(p + 1) * sub, :], preferred_element_type=jnp.float32)

    if last:
        @pl.when(step == pl.num_programs(0) - 1)
        def _():
            y = y_ref[0]
            quarter = sums.shape[1] // 4
            own_ref[...] = sums[:, pl.ds(pl.multiple_of(y * quarter, quarter), quarter)]
            peak = jnp.max(jnp.abs(sums[...]), axis=1, keepdims=True)
            level = jnp.ceil(jnp.log2(jnp.maximum(peak, 1e-30)) * levels)
            inv = 1.0 / step_of(level)
            for k in range(1, 4):
                to = (y + k) % 4
                v = sums[:, pl.ds(pl.multiple_of(to * quarter, quarter), quarter)] * inv
                far[k - 1][0:centers, :] = jnp.round(v).astype(jnp.int32).astype(jnp.int16)
            tot = jnp.sum(counts[...], axis=1, keepdims=True) * 4.0
            high = jnp.floor(tot)
            low = jnp.round((tot - high) * fine)
            col = lax.broadcasted_iota(jnp.int32, counts.shape, 1)
            notes = jnp.where(col == 0, high, jnp.where(col == 1, low, jnp.where(col == 2, level, 0.0)))
            turned = notes.T[0:16, :].astype(jnp.int32).astype(jnp.int16)
            for g in range(4):
                part = turned[:, g * each:(g + 1) * each]
                home_ref[g * 16:(g + 1) * 16, :] = part
                for k in range(3):
                    far[k][centers + g * 16:centers + (g + 1) * 16, :] = part


def merge_kernel(own_ref, home_ref, *refs):
    far, out_ref = refs[:3], refs[3]
    each = own_ref.shape[0]
    m = 4 * each
    g = pl.program_id(0)
    rows = pl.ds(pl.multiple_of(g * each, each), each)
    marks = pl.ds(pl.multiple_of(m + g * 16, 16), 16)
    notes = [home_ref[...]] + [f[marks, :].astype(jnp.int32).astype(jnp.float32) for f in far]
    turned = jnp.concatenate(notes * 2, axis=0).T
    total = 1.0
    summed = own_ref[...]
    for k in range(4):
        at = 16 * k
        total = total + (turned[:, at:at + 1] + turned[:, at + 1:at + 2] * (1.0 / fine)) * 0.25
        if k:
            summed = summed + far[k - 1][rows, :].astype(jnp.int32).astype(jnp.float32) * step_of(turned[:, at + 2:at + 3])
    out_ref[...] = summed / total


def merge(own, home, far):
    m, quarter = own.shape
    block = pl.BlockSpec((m // 4, quarter), lambda i: (i, 0))
    return pl.pallas_call(
        merge_kernel,
        grid=(4,),
        in_specs=[block, pl.BlockSpec((16, quarter), lambda i: (i, 0))] + [pl.BlockSpec(memory_space=pltpu.VMEM)] * 3,
        out_specs=block,
        out_shape=jax.ShapeDtypeStruct(own.shape, jnp.float32),
        compiler_params=pltpu.CompilerParams(dimension_semantics=("arbitrary",), vmem_limit_bytes=24 * 1024 * 1024),
    )(own, home, *far)


def pack_kernel(clusters, cut, keys_ref, map_ref, used_ref, x_ref, out_ref):
    owners, capacity = keys_ref.shape
    first = owners * pl.program_id(0)
    table = jnp.broadcast_to(map_ref[...], (owners, capacity))
    position = jnp.take_along_axis(table, keys_ref[...], axis=1)
    used = jnp.broadcast_to(used_ref[...], (owners, used_ref.shape[1]))
    mine = lax.broadcasted_iota(jnp.int32, used.shape, 1) == first + lax.broadcasted_iota(jnp.int32, used.shape, 0)
    limit = jnp.sum(jnp.where(mine, used, 0), axis=1, keepdims=True)
    live = lax.broadcasted_iota(jnp.int32, position.shape, 1) < limit
    codes = jnp.where(live, lax.rem(position, clusters), -1)
    edge = out_ref.shape[1] - 16
    out_ref[:, 0:edge, :] = x_ref[:, 0:edge, :]
    high = codes.astype(jnp.float32)
    wide = jnp.concatenate([high] * (x_ref.shape[2] // capacity), axis=1)
    row = lax.broadcasted_iota(jnp.int32, (16, x_ref.shape[2]), 0) + edge
    for j in range(owners):
        kept = x_ref[j, edge:edge + 16, :].astype(jnp.float32)
        out_ref[j, edge:edge + 16, :] = jnp.where(row < cut, kept, wide[j:j + 1, :]).astype(jnp.bfloat16)


def pack(blocks, keys, owner_map, used, clusters, cut, rows):
    owners, capacity, features = blocks.shape
    group = 8
    return pl.pallas_call(
        functools.partial(pack_kernel, clusters, cut),
        grid=(owners // group,),
        in_specs=[
            pl.BlockSpec((group, capacity), lambda i: (i, 0)),
            pl.BlockSpec((1, owner_map.shape[0]), lambda i: (0, 0)),
            pl.BlockSpec((1, owners), lambda i: (0, 0)),
            pl.BlockSpec((group, rows, features), lambda i: (i, 0, 0)),
        ],
        out_specs=pl.BlockSpec((group, rows, features), lambda i: (i, 0, 0)),
        out_shape=jax.ShapeDtypeStruct((owners, rows, features), blocks.dtype),
        compiler_params=pltpu.CompilerParams(dimension_semantics=("arbitrary",)),
    )(keys, owner_map.reshape(1, -1), used, blocks)


def assign(rows, codes, centers, csq, carry=None, y=None, tile=512, parts=2):
    n, d = rows.shape
    m = centers.shape[0]
    first, last = carry is None, y is not None
    f32 = jnp.float32
    resident = pl.BlockSpec(memory_space=pltpu.VMEM)
    whole = lambda shape: pl.BlockSpec(shape, lambda i, *_: (0,) * len(shape))
    in_specs = [pl.BlockSpec((1, tile), lambda i, *_: (0, i)), pl.BlockSpec((tile, d), lambda i, *_: (i, 0)),
                resident, resident]
    args = [codes, rows, centers, csq]
    if not first:
        in_specs += [pl.BlockSpec(memory_space=pl.ANY)] * 2
        args += list(carry)
    out_specs = [pl.BlockSpec((1, tile), lambda i, *_: (0, i))]
    outs = [jax.ShapeDtypeStruct((1, n), f32)]
    scratch = []
    if last:
        out_specs += [whole((m, d // 4))] + [whole((m + 64, d // 4))] * 3 + [whole((64, d // 4))]
        outs += [jax.ShapeDtypeStruct((m, d // 4), f32)] + [jax.ShapeDtypeStruct((m + 64, d // 4), jnp.int16)] * 3 + [jax.ShapeDtypeStruct((64, d // 4), jnp.int16)]
        scratch = [pltpu.VMEM((m, d), f32), pltpu.VMEM((m, 128), f32), pltpu.SemaphoreType.DMA((2,))]
        args = [y.reshape(1).astype(jnp.int32)] + args
    else:
        out_specs += [whole((m, d)), whole((m, 128))]
        outs += [jax.ShapeDtypeStruct((m, d), f32), jax.ShapeDtypeStruct((m, 128), f32)]
    return pl.pallas_call(
        functools.partial(assign_kernel, tile, parts, first, last),
        grid_spec=pltpu.PrefetchScalarGridSpec(num_scalar_prefetch=1 if last else 0, grid=(n // tile,), in_specs=in_specs,
            out_specs=out_specs, scratch_shapes=scratch),
        out_shape=outs,
        compiler_params=pltpu.CompilerParams(dimension_semantics=("arbitrary",), vmem_limit_bytes=60 * 1024 * 1024),
        cost_estimate=pl.CostEstimate(flops=4 * n * m * d, bytes_accessed=2 * n * d + 2 * m * d + 4 * m * d, transcendentals=n * m // 4),
    )(*args)


from jax.sharding import PartitionSpec as P

cut, extra = 88, 8
tiles = (1024, 1280)
parts = (2, 1)


def around(k, size):
    return [(i, (i + k) % size) for i in range(size)]


def body(embeddings, cluster_keys, owner_map, live_counts, sub_centroids):
    owners = lax.axis_size("clu")
    groups = lax.axis_size("row")
    slots, features = embeddings.shape
    capacity = slots // owners
    clusters_here, centers_each = sub_centroids.shape[:2]
    y = lax.axis_index("row").astype(jnp.int32)

    keys = cluster_keys.reshape(owners, capacity)
    blocks = embeddings.reshape(owners, capacity, features)
    centers = sub_centroids.reshape(clusters_here * centers_each, features)
    center_squares = jnp.sum(centers.astype(jnp.float32) ** 2, axis=1, keepdims=True) * inverse_temp
    row_squares = jnp.sum(blocks.astype(jnp.float32) ** 2, axis=2)
    share = lax.dynamic_slice_in_dim(centers, y * (features // groups), features // groups, 1)

    first = pack(blocks, keys, owner_map, live_counts, clusters_here, cut, cut + extra)
    second = blocks[:, cut:]
    second, center_squares, row_squares, share = lax.optimization_barrier(
        (second, center_squares, row_squares, share)
    )
    received = [
        lax.all_to_all(part, "clu", split_axis=0, concat_axis=0, tiled=True)
        for part in (first, second)
    ]
    codes_in = received[0][:, cut, :capacity].astype(jnp.int32)
    none = jnp.full((owners, extra), -1, jnp.int32)
    codes = (jnp.concatenate([codes_in[:, :cut], none], axis=1), codes_in[:, cut:])
    carry = None
    gains = []
    for i in range(2):
        count = received[i].shape[1]
        rows = received[i].reshape(owners * count, features)
        out = assign(rows, codes[i].reshape(1, owners * count), centers, center_squares, carry, y if i else None, tiles[i], parts[i])
        gains.append(out[0].reshape(owners, count))
        carry = out[1:]
    gains[0] = gains[0][:, :cut]
    own, far1, far2, far3, home = carry

    got2 = lax.ppermute(far2, "row", around(2, groups))
    got1 = lax.ppermute(far1, "row", around(1, groups))
    got3 = lax.ppermute(far3, "row", around(3, groups))
    returned = lax.all_to_all(jnp.concatenate(gains, axis=1), "clu", split_axis=0, concat_axis=0, tiled=True)
    updated = merge(own + share.astype(jnp.float32), home.astype(jnp.float32), (got1, got2, got3))
    new_centroids = updated.reshape(clusters_here, centers_each, features // groups)
    live = jnp.arange(capacity, dtype=jnp.int32)[None, :] < live_counts[0][:, None]
    row_costs = jnp.where(live, row_squares + returned, 0.0) * (1.0 / features)
    return new_centroids, row_costs.reshape(slots)


def solution(mesh):
    return jax.shard_map(
        body,
        mesh=mesh,
        in_specs=(
            P(("clu", "row"), None),
            P(("clu", "row")),
            P(),
            P(("clu", "row"), None),
            P("clu", None, None),
        ),
        out_specs=(P("clu", None, "row"), P(("clu", "row"))),
        check_vma=False,
    )
```
